32 devices in a mesh: tok: 16 (over z, y, core), head: 2 (over x).
Axes of the slice: x: 2, y: 2, z: 4, core: 2. Of those that a mesh axis runs over, the one named last changes fastest.
Arguments:
- tokens: bfloat16 [2048, 768], P('tok', 'head'), may hold values from -64 to 64
- view_ids: int32 [2048], P('tok'), may hold values from 0 to 4, never falling along the last dimension, each value on 1 to 512 neighbouring positions
- query_weight: bfloat16 [768, 768], P(None, 'head'), may hold values from -0.21875 to 0.21875
- key_weight: bfloat16 [768, 768], P(None, 'head'), may hold values from -0.4375 to 0.4375
- value_weight: bfloat16 [768, 768], P(None, 'head'), may hold values from -0.21875 to 0.21875
- out_weight: bfloat16 [768, 768], P('head'), may hold values from -0.21875 to 0.21875
- rate_weight: bfloat16 [768, 4], P(None, 'head'), may hold values from -0.21875 to 0.21875
- fast_gate: float32 [4, 192, 384], P('head'), may hold values from -0.4375 to 0.4375
- fast_up: float32 [4, 192, 384], P('head'), may hold values from -0.4375 to 0.4375
- fast_down: float32 [4, 192, 384], P('head'), may hold values from -0.3125 to 0.3125
- step_size: float32 [4], P('head'), may hold values from 1 to 3
Outputs:
- layer_out: bfloat16 [2048, 768], P('tok', 'head')
The draws below stay inside these ranges and needn't reach their ends.
Inputs may be any that keep to these rules, and one draw needn't show every extreme that they name: `view_ids`: Non-decreasing along the tokens; every view number appears, on one contiguous run of 1 to 512 tokens, and some view has exactly 512.
All inputs are finite; a program needn't handle non-finite values.
Results may differ from the reference program's by a relative error of at most 0.014.
The reference program's roundings to bfloat16 on the way (of `lowered`, `product`, `error`, `fresh` and `mixed`) count: a program that leaves them out, or rounds other values in their place, can miss the bound.
Values may be sent and summed in bfloat16 or wider, within the bound.
A program may use at most 64 MiB of HBM per device.

```python
import math
import jax
import jax.numpy as jnp
import numpy as np
from jax import lax

D = 768
HEADS = 4
FH = 384
NS_STEPS = 5
TOK_DEV = 128
DH = 192
TOKENS = 2048
VIEW_SPAN = 4
VIEWS = 5
N_TOK = 16


def draw_tokens(key, part):
    first_key = jax.random.fold_in(jax.random.fold_in(key, 11), 0)
    base = jnp.clip(jax.random.normal(first_key, (TOKENS, D), jnp.float32), -6.0, 6.0)
    return base.astype(jnp.bfloat16)


def steps_of(own_key, dims, shards, smallest, high):
    gain = 1.0
    for position, parts in shards:
        heights = jax.random.uniform(jax.random.fold_in(jax.random.fold_in(own_key, 6), position), (parts,), jnp.float32, smallest / len(shards), high / len(shards))
        gain = gain * jnp.repeat(jnp.exp(heights), dims[position] // parts).reshape((-1,) + (1,) * (len(dims) - 1 - position))
    return gain


def split_up(amount, total, most, lean):
    portions = [(1 << 20) // math.isqrt(rank ** lean) + 1 for rank in range(2, amount + 1)]
    rest, given = total - most - (amount - 1), [1] * (amount - 1)
    while rest > 0:
        movable = [i for i in range(amount - 1) if given[i] < most]
        pool, remaining = sum([portions[i] for i in movable]), rest
        for i in movable:
            addition = min(most - given[i], max(1, remaining * portions[i] // pool), rest)
            given[i] = given[i] + addition
            rest = rest - addition
    return np.array([most] + given)


def uneven_parts(stream_key, amount, total, bound, slope):
    if amount == 2:
        one = jax.random.randint(stream_key, (), max(1, total - bound), min(bound, total - 1) + 1)
        return jnp.stack([one, total - one])
    tallies = jnp.asarray(split_up(amount, total, bound, slope), jnp.int32)
    couples = (amount - 1) // 2
    giver, receiver = tallies[1:1 + 2 * couples:2], tallies[2:2 + 2 * couples:2]
    slack = jnp.minimum(giver - 1, bound - receiver)
    moved = jax.random.randint(jax.random.fold_in(stream_key, 1), (couples,), 0, 1 << 20) % (slack + 1)
    tallies = tallies.at[1:1 + 2 * couples:2].set(giver - moved).at[2:2 + 2 * couples:2].set(receiver + moved)
    return tallies[jax.random.permutation(jax.random.fold_in(stream_key, 2), amount)]


def bell_draw(own_key, dims, scale, reach, pieces=(), held_as=jnp.bfloat16):
    loudness = steps_of(own_key, dims, pieces, -0.22, 0.18) if pieces else 1.0
    drawn = jax.random.normal(own_key, dims, jnp.float32) * scale * loudness
    return jnp.minimum(jnp.maximum(drawn, -reach), reach).astype(held_as)


def setup_inputs(seed: int = 0) -> dict:
    streams_of = jax.random.split(jax.random.key(seed), 12)
    tokens = draw_tokens(jax.random.fold_in(streams_of[11], 71), 0)
    view_ids = jnp.searchsorted(jnp.cumsum(uneven_parts(streams_of[1], VIEWS, TOKENS, VIEW_SPAN * TOK_DEV, 0)), jnp.arange(TOKENS), side="right").astype(jnp.int32)
    query_weight = bell_draw(streams_of[2], (D, D), D ** -0.5, 0.21875, ((1, 2),))
    key_weight = bell_draw(streams_of[3], (D, D), (D // 4) ** -0.5, 0.4375, ((1, 2),))
    value_weight = bell_draw(streams_of[4], (D, D), D ** -0.5, 0.21875, ((1, 2),))
    out_weight = bell_draw(streams_of[5], (D, D), D ** -0.5, 0.21875, ((0, 2),))
    rate_weight = bell_draw(streams_of[6], (D, HEADS), D ** -0.5, 0.21875, ((1, 2),))
    fast_gate = bell_draw(streams_of[7], (HEADS, DH, FH), DH ** -0.5, 0.4375, ((0, 2),), jnp.float32)
    fast_up = bell_draw(streams_of[8], (HEADS, DH, FH), DH ** -0.5, 0.4375, ((0, 2),), jnp.float32)
    fast_down = bell_draw(streams_of[9], (HEADS, DH, FH), FH ** -0.5, 0.3125, ((0, 2),), jnp.float32)
    step_size = jnp.clip(jnp.exp(math.log(3.0) - 1.0986123 * jax.random.uniform(streams_of[10], (HEADS,), jnp.float32) ** steps_of(streams_of[10], (HEADS,), ((0, 2),), -0.2, 0.2)), 1.0, 3.0)
    return dict(tokens=tokens, view_ids=view_ids, query_weight=query_weight, key_weight=key_weight, value_weight=value_weight, out_weight=out_weight, rate_weight=rate_weight, fast_gate=fast_gate, fast_up=fast_up, fast_down=fast_down, step_size=step_size)


newton_a = 3.4445
newton_b = -4.775
newton_c = 2.0315
epsilon = 1e-06
masked_score = -1e+30

def normalize(values):
    widened = values.astype(jnp.float32)
    scale = lax.rsqrt(lax.optimization_barrier(jnp.mean(widened * widened, axis=-1, keepdims=True)) + epsilon)
    return (widened * scale).astype(jnp.bfloat16)

def orthogonalize(matrix):
    length = jnp.sqrt(lax.optimization_barrier(jnp.sum(matrix * matrix, axis=(-2, -1), keepdims=True)))
    current = matrix / (length + epsilon)
    for ns_step in range(NS_STEPS):
        square = jnp.einsum('...ik,...jk->...ij', current, current, precision=lax.Precision.HIGHEST)
        mixer = newton_b * square + newton_c * jnp.einsum('...ik,...kj->...ij', square, square, precision=lax.Precision.HIGHEST)
        current = newton_a * current + jnp.einsum('...ik,...kj->...ij', mixer, current, precision=lax.Precision.HIGHEST)
    return current

def fast_terms(keys_n, values, rates, lowered):
    widened = keys_n.astype(jnp.float32)
    gate = jnp.einsum('thd,hdf->thf', widened, lowered[:, 0].astype(jnp.float32))
    upward = jnp.einsum('thd,hdf->thf', widened, lowered[:, 1].astype(jnp.float32))
    active = jax.nn.silu(gate)
    product = (active * upward).astype(jnp.bfloat16)
    error = (-rates[:, :, None] * values.astype(jnp.float32)).astype(jnp.bfloat16)
    grad_down = jnp.einsum('thf,thd->hdf', product.astype(jnp.float32), error.astype(jnp.float32))
    back = jnp.einsum('thd,hdf->thf', error.astype(jnp.float32), lowered[:, 2].astype(jnp.float32))
    logistic = jax.nn.sigmoid(gate)
    grad_gate_in = (back * upward * logistic * (1.0 + gate * (1.0 - logistic))).astype(jnp.bfloat16)
    grad_up_in = (back * active).astype(jnp.bfloat16)
    grad_gate = jnp.einsum('thd,thf->hdf', widened, grad_gate_in.astype(jnp.float32))
    grad_up = jnp.einsum('thd,thf->hdf', widened, grad_up_in.astype(jnp.float32))
    return jnp.stack((grad_gate, grad_up, grad_down), 1)

def apply_fast(queries_n, fresh):
    widened = queries_n.astype(jnp.float32)
    gate = jnp.einsum('thd,hdf->thf', widened, fresh[:, 0].astype(jnp.float32))
    upward = jnp.einsum('thd,hdf->thf', widened, fresh[:, 1].astype(jnp.float32))
    product = (jax.nn.silu(gate) * upward).astype(jnp.bfloat16)
    return jnp.einsum('thf,hdf->thd', product.astype(jnp.float32), fresh[:, 2].astype(jnp.float32))

def attend(query_rows, key_rows, value_rows, query_view, key_view):
    scores = jnp.einsum('qhd,khd->hqk', query_rows.astype(jnp.float32), key_rows.astype(jnp.float32))
    scores = scores * query_rows.shape[2] ** (-0.5)
    allowed = (query_view[:, None] == key_view[None, :])[None]
    scores = jnp.where(allowed, scores, masked_score)
    peak = lax.optimization_barrier(jnp.max(scores, axis=-1, keepdims=True))
    weights = jnp.exp(scores - peak)
    weights = (weights / lax.optimization_barrier(jnp.sum(weights, axis=-1, keepdims=True))).astype(jnp.bfloat16)
    return jnp.einsum('hqk,khd->qhd', weights.astype(jnp.float32), value_rows.astype(jnp.float32))

def reference(tokens, view_ids, query_weight, key_weight, value_weight, out_weight, rate_weight, fast_gate, fast_up, fast_down, step_size):
    head_width = D // HEADS
    queries = jnp.dot(tokens, query_weight, preferred_element_type=jnp.float32).astype(jnp.bfloat16).reshape(TOKENS, HEADS, head_width)
    keys = jnp.dot(tokens, key_weight, preferred_element_type=jnp.float32).astype(jnp.bfloat16).reshape(TOKENS, HEADS, head_width)
    values = jnp.dot(tokens, value_weight, preferred_element_type=jnp.float32).astype(jnp.bfloat16).reshape(TOKENS, HEADS, head_width)
    rates = jax.nn.softplus(jnp.dot(tokens, rate_weight, preferred_element_type=jnp.float32))
    positions = jnp.arange(TOKENS, dtype=jnp.int32)
    rates = rates * (positions < 3 * TOKENS // 4).astype(jnp.float32)[:, None]
    keys_n = normalize(keys)
    queries_n = normalize(queries)
    master = jnp.stack((fast_gate, fast_up, fast_down), 1)
    lowered = master.astype(jnp.bfloat16)

    def slice_block(array, start):
        return lax.dynamic_slice_in_dim(array, start, TOK_DEV, 0)

    def accumulate(carry, block_index):
        start = block_index * TOK_DEV
        term = fast_terms(slice_block(keys_n, start), slice_block(values, start), slice_block(rates, start), lowered)
        return (carry + term, None)
    total, unused = lax.scan(accumulate, jnp.zeros(master.shape, jnp.float32), jnp.arange(N_TOK, dtype=jnp.int32))
    fresh = (master - step_size[:, None, None, None] * orthogonalize(total)).astype(jnp.bfloat16)
    margin_rows = VIEW_SPAN * TOK_DEV
    window_rows = (2 * VIEW_SPAN + 1) * TOK_DEV
    blank = jnp.zeros((margin_rows, HEADS, head_width), jnp.bfloat16)
    padded_keys = jnp.concatenate((blank, keys, blank), 0)
    padded_values = jnp.concatenate((blank, values, blank), 0)
    blank_views = jnp.full((margin_rows,), -1, jnp.int32)
    padded_views = jnp.concatenate((blank_views, view_ids.astype(jnp.int32), blank_views), 0)

    def output_block(block_index):
        start = block_index * TOK_DEV
        near_keys = lax.dynamic_slice_in_dim(padded_keys, start, window_rows, 0)
        near_values = lax.dynamic_slice_in_dim(padded_values, start, window_rows, 0)
        near_views = lax.dynamic_slice_in_dim(padded_views, start, window_rows, 0)
        attended = attend(slice_block(queries, start), near_keys, near_values, slice_block(view_ids, start), near_views)
        applied = apply_fast(slice_block(queries_n, start), fresh)
        mixed = (attended + applied).astype(jnp.bfloat16).reshape(TOK_DEV, D)
        return jnp.dot(mixed, out_weight, preferred_element_type=jnp.float32).astype(jnp.bfloat16)
    return lax.map(output_block, jnp.arange(N_TOK, dtype=jnp.int32)).reshape(TOKENS, D)
```

```python
import jax
import jax.numpy as jnp
from jax import lax
from jax.experimental import pallas as pl
from jax.experimental.pallas import tpu as pltpu
from jax.sharding import PartitionSpec as P

NS_STEPS = 5
MATRICES = 3
newton_a = 3.4445
newton_b = -4.775
newton_c = 2.0315
epsilon = 1e-06
masked_score = -1e30
F32, BF16 = jnp.float32, jnp.bfloat16
MESH = pl.DeviceIdType.MESH

NN = (((1,), (0,)), ((), ()))
NT = (((1,), (1,)), ((), ()))
TN = (((0,), (0,)), ((), ()))


def mul(a, b, dims=NN):
    return lax.dot_general(a, b, dims, preferred_element_type=F32)


def split(x):
    high = x.astype(BF16)
    return high, (x - high.astype(F32)).astype(BF16)


def mul3(a, b, dims=NN):
    return mul(a[0], b[0], dims) + (mul(a[0], b[1], dims) + mul(a[1], b[0], dims))


def orthogonalize(matrix):
    length = jnp.sqrt(jnp.sum(matrix * matrix, keepdims=True))
    current = matrix / (length + epsilon)
    for _ in range(NS_STEPS):
        parts = split(current)
        square = mul3(parts, parts, NT)
        square_parts = split(square)
        mixer = newton_b * square + newton_c * mul3(square_parts, square_parts)
        current = newton_a * current + mul3(split(mixer), parts)
    return current


def normalize(values):
    widened = values.astype(F32)
    scale = lax.rsqrt(jnp.mean(widened * widened, axis=-1, keepdims=True) + epsilon)
    return (widened * scale).astype(BF16)


def sigmoid(x):
    return 1.0 / (1.0 + jnp.exp(-x))


def make_kernel(tok_count, span, contributors):
    chips = tok_count // 2

    def kernel(
        tokens, views, query_hbm, key_hbm, value_hbm, out_hbm, rate_w, gate_hbm, up_hbm, down_hbm, step,
        result,
        query_w, key_w, value_w, out_w, fast, load_sem,
        other_tokens, tok_send, tok_recv,
        mate_out, both, both_views, view_out, mate_send, mate_recv,
        window, window_send, window_recv,
        partial, arrived, own_total, reduce_send, reduce_recv,
        other_out_w, out_send, out_recv,
        fresh, fresh_out, fresh_send, fresh_recv,
        mixed_out, mixed_in, mixed_send, mixed_recv,
    ):
        rows, half = tokens.shape
        width = fast.shape[1]
        t = lax.axis_index("tok")
        x = lax.axis_index("head")
        core, chip = lax.rem(t, 2), lax.div(t, 2)
        mate, other = t + 1 - 2 * core, 1 - x

        def tok_of(which):
            return 2 * which + core

        barrier = pltpu.get_barrier_semaphore()
        group = [(mate, x), (t, other), (mate, other)]
        for who in group:
            pl.semaphore_signal(barrier, inc=1, device_id=who, device_id_type=MESH)

        @pl.loop(1, chips)
        def _(k):
            pl.semaphore_signal(
                barrier, inc=1, device_id=(tok_of(lax.rem(chip + k, chips)), x), device_id_type=MESH
            )

        loads = [
            pltpu.make_async_copy(src, dst, load_sem.at[i])
            for i, (src, dst) in enumerate(
                (
                    (key_hbm, key_w),
                    (value_hbm, value_w),
                    (query_hbm, query_w),
                    (gate_hbm.at[core], fast.at[0]),
                    (up_hbm.at[core], fast.at[1]),
                    (down_hbm.at[core], fast.at[2]),
                    (out_hbm, out_w),
                )
            )
        ]
        for load in loads:
            load.start()

        def remote(src, dst, send, recv, who):
            return pltpu.make_async_remote_copy(
                src_ref=src, dst_ref=dst, send_sem=send, recv_sem=recv, device_id=who, device_id_type=MESH
            )

        own_view = jnp.broadcast_to(views[...].astype(F32), (16, rows)).astype(BF16)
        view_out[...] = own_view
        both_views[:, pl.ds(pl.multiple_of(core * rows, 128), rows)] = own_view

        pl.semaphore_wait(barrier, len(group) + chips - 1)
        token_copy = remote(tokens, other_tokens, tok_send, tok_recv, (t, other))
        token_copy.start()
        view_copy = remote(
            view_out,
            both_views.at[:, pl.ds(pl.multiple_of(core * rows, 128), rows)],
            mate_send.at[1],
            mate_recv.at[1],
            (mate, x),
        )
        view_copy.start()

        own_rows = pl.ds(pl.multiple_of(x * half, 128), half)
        far_rows = pl.ds(pl.multiple_of(other * half, 128), half)
        mine = tokens[...]
        for load in loads[:3]:
            load.wait()
        keys = mul(mine, key_w[own_rows, :])
        values = mul(mine, value_w[own_rows, :])
        queries = mul(mine, query_w[own_rows, :])
        rates = mul(mine, rate_w[own_rows, :])
        token_copy.wait_recv()
        far = other_tokens[...]
        keys = (keys + mul(far, key_w[far_rows, :])).astype(BF16)
        values = (values + mul(far, value_w[far_rows, :])).astype(BF16)
        rates = rates + mul(far, rate_w[far_rows, :])
        rates = jnp.maximum(rates, 0.0) + jnp.log1p(jnp.exp(-jnp.abs(rates)))
        rates = rates * jnp.where(chip < contributors, 1.0, 0.0)
        queries = (queries + mul(far, query_w[far_rows, :])).astype(BF16)

        def packed(head):
            cols = slice(head * width, (head + 1) * width)
            error = (-rates[:, head : head + 1] * values[:, cols].astype(F32)).astype(BF16)
            return jnp.concatenate((keys[:, cols], values[:, cols], queries[:, cols], error), 1)

        first, second = packed(0), packed(1)
        mate_out[...] = jnp.where(core == 0, second, first)
        core_rows = pl.ds(pl.multiple_of(core * rows, 128), rows)
        mate_rows = pl.ds(pl.multiple_of((1 - core) * rows, 128), rows)
        mate_copy = remote(mate_out, both.at[core_rows, :], mate_send.at[0], mate_recv.at[0], (mate, x))
        mate_copy.start()
        both[core_rows, :] = jnp.where(core == 0, first, second)
        for load in loads[3:]:
            load.wait()
        out_copy = remote(
            out_w.at[:, pl.ds(pl.multiple_of(other * half, 128), half)], other_out_w, out_send, out_recv, (t, other)
        )
        out_copy.start()
        lowered = [fast[m].astype(BF16) for m in range(MATRICES)]
        remote(mate_out, both.at[mate_rows, :], mate_send.at[0], mate_recv.at[0], (mate, x)).wait_recv()
        remote(
            view_out,
            both_views.at[:, pl.ds(pl.multiple_of((1 - core) * rows, 128), rows)],
            mate_send.at[1],
            mate_recv.at[1],
            (mate, x),
        ).wait_recv()

        span_rows = 2 * rows
        window[span, 0:span_rows, :] = both[:, 0 : 2 * width]
        window[span, span_rows : span_rows + 16, :] = jnp.concatenate(
            (both_views[...], jnp.zeros((16, 2 * width - span_rows), BF16)), 1
        )

        def reduce_copy(m):
            return remote(
                partial.at[m],
                arrived.at[chip],
                reduce_send.at[m],
                reduce_recv.at[chip],
                (tok_of(core * MATRICES + m), x),
            )

        def hand_over(m, value):
            partial[m] = value.astype(BF16)
            owner = core * MATRICES + m

            @pl.when(owner == chip)
            def _():
                own_total[...] = value

            @pl.when(owner != chip)
            def _():
                reduce_copy(m).start()

        @pl.when(chip < contributors)
        def _():
            keys_n = normalize(both[:, 0:width])
            error = both[:, 3 * width : 4 * width]
            gate = mul(keys_n, lowered[0])
            upward = mul(keys_n, lowered[1])
            logistic = sigmoid(gate)
            active = gate * logistic
            hand_over(2, mul(error, (active * upward).astype(BF16), TN))
            back = mul(error, lowered[2])
            hand_over(1, mul(keys_n, (back * active).astype(BF16), TN))
            grad_gate = (back * upward * logistic * (1.0 + gate * (1.0 - logistic))).astype(BF16)
            hand_over(0, mul(keys_n, grad_gate, TN))

        def window_copy(offset):
            return remote(
                window.at[span],
                window.at[span - offset],
                window_send.at[span + offset],
                window_recv.at[span - offset],
                (tok_of(chip + offset), x),
            )

        offsets = [o for o in range(-span, span + 1) if o]
        for offset in offsets:
            inside = (chip + offset >= 0) & (chip + offset < chips)

            @pl.when(inside)
            def _(offset=offset):
                window_copy(offset).start()

            @pl.when(jnp.logical_not(inside))
            def _(offset=offset):
                window[span + offset, 0:span_rows, :] = jnp.zeros((span_rows, 2 * width), BF16)
                window[span + offset, span_rows : span_rows + 16, :] = jnp.full((16, 2 * width), -1.0, BF16)

        index = chip - core * MATRICES
        owns = (index >= 0) & (index < MATRICES)

        def fresh_copy(k):
            return remote(
                fresh_out,
                fresh.at[index],
                fresh_send.at[k],
                fresh_recv.at[index],
                (tok_of(lax.rem(chip + k, chips)), x),
            )

        @pl.when(owns)
        def _():
            @pl.loop(1, contributors)
            def _(k):
                source = lax.rem(chip + k, contributors)
                remote(
                    partial.at[0], arrived.at[source], reduce_send.at[0], reduce_recv.at[source], (mate, x)
                ).wait_recv()
                own_total[...] += arrived[source].astype(F32)

            pace = jnp.where(core == 0, step[0], step[1])
            updated = (fast[index] - pace * orthogonalize(own_total[...])).astype(BF16)
            fresh_out[...] = updated

            @pl.loop(1, chips)
            def _(k):
                fresh_copy(k).start()

            fresh[index] = updated

        own_queries = both[:, 2 * width : 3 * width]
        own_views = both_views[0:1, :].astype(F32)
        diagonal = lax.broadcasted_iota(jnp.int32, (span_rows, span_rows), 0) == lax.broadcasted_iota(
            jnp.int32, (span_rows, span_rows), 1
        )
        column_views = jnp.sum(jnp.where(diagonal, own_views, 0.0), axis=1, keepdims=True)
        scores = []
        for offset in sorted(range(-span, span + 1), key=abs):
            slot = span + offset
            if offset:

                @pl.when((chip + offset >= 0) & (chip + offset < chips))
                def _(slot=slot):
                    remote(
                        window.at[span], window.at[slot], window_send.at[slot], window_recv.at[slot], (mate, x)
                    ).wait_recv()

            score = mul(own_queries, window[slot, 0:span_rows, 0:width], NT) * width ** (-0.5)
            near = window[slot, span_rows : span_rows + 16, 0:span_rows].astype(F32)[0:1, :]
            scores.append((slot, jnp.where(column_views == near, score, masked_score)))
        peak = scores[0][1].max(axis=1, keepdims=True)
        for _, score in scores[1:]:
            peak = jnp.maximum(peak, score.max(axis=1, keepdims=True))
        weights = [(slot, jnp.exp(score - peak)) for slot, score in scores]
        denominator = sum(w.sum(axis=1, keepdims=True) for _, w in weights)
        attended = sum(
            mul((w / denominator).astype(BF16), window[slot, 0:span_rows, width : 2 * width]) for slot, w in weights
        )

        queries_n = normalize(own_queries)
        for m in range(MATRICES):

            @pl.when(chip != core * MATRICES + m)
            def _(m=m):
                remote(fresh_out, fresh.at[m], fresh_send.at[0], fresh_recv.at[m], (mate, x)).wait_recv()

        gate = mul(queries_n, fresh[0])
        upward = mul(queries_n, fresh[1])
        product = (gate * sigmoid(gate) * upward).astype(BF16)
        mixed = (attended + mul(product, fresh[2], NT)).astype(BF16)

        mixed_out[...] = mixed
        copies = [
            remote(mixed_out.at[where, :], mixed_in.at[i], mixed_send.at[i], mixed_recv.at[i], who)
            for i, (where, who) in enumerate(
                ((mate_rows, group[0]), (core_rows, group[1]), (mate_rows, group[2]))
            )
        ]
        for i in (1, 2, 0):
            copies[i].start()
        out_copy.wait_recv()
        kept = mixed_out[core_rows, :]
        copies[0].wait_recv()

        def side_by_side(a, b):
            return jnp.where(core == 0, jnp.concatenate((a, b), 1), jnp.concatenate((b, a), 1))

        total = mul(side_by_side(kept, mixed_in[0]), out_w[:, pl.ds(pl.multiple_of(x * half, 128), half)])
        copies[1].wait_recv()
        copies[2].wait_recv()
        total = total + mul(side_by_side(mixed_in[1], mixed_in[2]), other_out_w[...])
        result[...] = total.astype(BF16)

        token_copy.wait_send()
        view_copy.wait_send()
        mate_copy.wait_send()
        out_copy.wait_send()
        for copy in copies:
            copy.wait_send()

        @pl.when(chip < contributors)
        def _():
            for m in range(MATRICES):

                @pl.when(chip != core * MATRICES + m)
                def _(m=m):
                    reduce_copy(m).wait_send()

        for offset in offsets:

            @pl.when((chip + offset >= 0) & (chip + offset < chips))
            def _(offset=offset):
                window_copy(offset).wait_send()

        @pl.when(owns)
        def _():
            @pl.loop(1, chips)
            def _(k):
                fresh_copy(k).wait_send()

    return kernel


def body(
    tokens, view_ids, query_weight, key_weight, value_weight, out_weight,
    rate_weight, fast_gate, fast_up, fast_down, step_size,
):
    tok_count = lax.axis_size("tok")
    chips = tok_count // 2
    span = min(8, tok_count // 4) // 2
    contributors = 3 * tok_count // 8
    rows, half = tokens.shape
    width, hidden = fast_gate.shape[1:]
    slots = 2 * span + 1
    vmem = pl.BlockSpec(memory_space=pltpu.VMEM)
    anywhere = pl.BlockSpec(memory_space=pl.ANY)
    dma = pltpu.SemaphoreType.DMA
    matrix = (width, hidden)
    return pl.pallas_call(
        make_kernel(tok_count, span, contributors),
        out_shape=jax.ShapeDtypeStruct((rows, half), BF16),
        in_specs=[vmem, vmem, anywhere, anywhere, anywhere, anywhere, vmem, anywhere, anywhere, anywhere,
                  pl.BlockSpec(memory_space=pltpu.SMEM)],
        out_specs=vmem,
        scratch_shapes=[
            pltpu.VMEM(query_weight.shape, BF16),
            pltpu.VMEM(key_weight.shape, BF16),
            pltpu.VMEM(value_weight.shape, BF16),
            pltpu.VMEM(out_weight.shape, BF16),
            pltpu.VMEM((MATRICES,) + matrix, F32),
            dma((7,)),
            pltpu.VMEM((rows, half), BF16),
            dma,
            dma,
            pltpu.VMEM((rows, 4 * width), BF16),
            pltpu.VMEM((2 * rows, 4 * width), BF16),
            pltpu.VMEM((16, 2 * rows), BF16),
            pltpu.VMEM((16, rows), BF16),
            dma((2,)),
            dma((2,)),
            pltpu.VMEM((slots, 2 * rows + 16, 2 * width), BF16),
            dma((slots,)),
            dma((slots,)),
            pltpu.VMEM((MATRICES,) + matrix, BF16),
            pltpu.VMEM((contributors,) + matrix, BF16),
            pltpu.VMEM(matrix, F32),
            dma((MATRICES,)),
            dma((contributors,)),
            pltpu.VMEM((half, half), BF16),
            dma,
            dma,
            pltpu.VMEM((MATRICES,) + matrix, BF16),
            pltpu.VMEM(matrix, BF16),
            dma((chips,)),
            dma((MATRICES,)),
            pltpu.VMEM((2 * rows, width), BF16),
            pltpu.VMEM((3, rows, width), BF16),
            dma((3,)),
            dma((3,)),
        ],
        compiler_params=pltpu.CompilerParams(
            collective_id=0, has_side_effects=True, vmem_limit_bytes=48 * 1024 * 1024
        ),
    )(
        tokens, view_ids.reshape(1, rows), query_weight, key_weight, value_weight, out_weight,
        rate_weight, fast_gate, fast_up, fast_down, step_size,
    )


def solution(mesh):
    placed = (
        P("tok", "head"),
        P("tok"),
        P(None, "head"),
        P(None, "head"),
        P(None, "head"),
        P("head", None),
        P(None, "head"),
        P("head", None, None),
        P("head", None, None),
        P("head", None, None),
        P("head"),
    )
    return jax.shard_map(
        body, mesh=mesh, in_specs=placed, out_specs=P("tok", "head"), check_vma=False
    )
```

```python
import jax
import jax.numpy as jnp
from jax import lax
from jax.experimental import pallas as pl
from jax.experimental.pallas import tpu as pltpu
from jax.sharding import PartitionSpec as P

NS_STEPS = 5
MATRICES = 3
newton_a = 3.4445
newton_b = -4.775
newton_c = 2.0315
epsilon = 1e-06
masked_score = -1e30
F32, BF16 = jnp.float32, jnp.bfloat16
MESH = pl.DeviceIdType.MESH

NN = (((1,), (0,)), ((), ()))
NT = (((1,), (1,)), ((), ()))
TN = (((0,), (0,)), ((), ()))


def mul(a, b, dims=NN):
    return lax.dot_general(a, b, dims, preferred_element_type=F32)


def split(x):
    high = x.astype(BF16)
    return high, (x - high.astype(F32)).astype(BF16)


def mul3(a, b, dims=NN):
    return mul(a[0], b[0], dims) + (mul(a[0], b[1], dims) + mul(a[1], b[0], dims))


def orthogonalize(matrix):
    length = jnp.sqrt(jnp.sum(matrix * matrix, keepdims=True))
    current = matrix / (length + epsilon)
    for _ in range(NS_STEPS):
        parts = split(current)
        square = mul3(parts, parts, NT)
        square_parts = split(square)
        mixer = newton_b * square + newton_c * mul3(square_parts, square_parts)
        current = newton_a * current + mul3(split(mixer), parts)
    return current


def normalize(values):
    widened = values.astype(F32)
    scale = lax.rsqrt(jnp.mean(widened * widened, axis=-1, keepdims=True) + epsilon)
    return (widened * scale).astype(BF16)


def sigmoid(x):
    return 1.0 / (1.0 + jnp.exp(-x))


def make_kernel(tok_count, span, contributors):
    chips = tok_count // 2

    def kernel(
        tokens, views, query_hbm, key_hbm, value_hbm, out_hbm, rate_w, gate_hbm, up_hbm, down_hbm, step,
        result,
        query_w, key_w, value_w, out_w, fast, load_sem,
        other_tokens, tok_send, tok_recv,
        mate_out, both, both_views, view_out, mate_send, mate_recv,
        window, window_send, window_recv,
        partial, arrived, own_total, reduce_send, reduce_recv,
        other_out_w, out_send, out_recv,
        fresh, forward_send, fresh_send, fresh_recv,
        mixed_out, mixed_in, mixed_send, mixed_recv,
    ):
        rows, half = tokens.shape
        width = fast.shape[1]
        t = lax.axis_index("tok")
        x = lax.axis_index("head")
        core, chip = lax.rem(t, 2), lax.div(t, 2)
        mate, other = t + 1 - 2 * core, 1 - x

        def tok_of(which):
            return 2 * which + core

        barrier = pltpu.get_barrier_semaphore()
        group = [(mate, x), (t, other), (mate, other)]
        for who in group:
            pl.semaphore_signal(barrier, inc=1, device_id=who, device_id_type=MESH)

        @pl.loop(1, chips)
        def _(k):
            pl.semaphore_signal(
                barrier, inc=1, device_id=(tok_of(lax.rem(chip + k, chips)), x), device_id_type=MESH
            )

        loads = [
            pltpu.make_async_copy(src, dst, load_sem.at[i])
            for i, (src, dst) in enumerate(
                (
                    (key_hbm, key_w),
                    (value_hbm, value_w),
                    (query_hbm, query_w),
                    (gate_hbm.at[core], fast.at[0]),
                    (up_hbm.at[core], fast.at[1]),
                    (down_hbm.at[core], fast.at[2]),
                    (out_hbm, out_w),
                )
            )
        ]
        for load in loads:
            load.start()

        def remote(src, dst, send, recv, who):
            return pltpu.make_async_remote_copy(
                src_ref=src, dst_ref=dst, send_sem=send, recv_sem=recv, device_id=who, device_id_type=MESH
            )

        own_view = jnp.broadcast_to(views[...].astype(F32), (16, rows)).astype(BF16)
        view_out[...] = own_view
        both_views[:, pl.ds(pl.multiple_of(core * rows, 128), rows)] = own_view

        pl.semaphore_wait(barrier, len(group) + chips - 1)
        token_copy = remote(tokens, other_tokens, tok_send, tok_recv, (t, other))
        token_copy.start()
        view_copy = remote(
            view_out,
            both_views.at[:, pl.ds(pl.multiple_of(core * rows, 128), rows)],
            mate_send.at[1],
            mate_recv.at[1],
            (mate, x),
        )
        view_copy.start()

        own_rows = pl.ds(pl.multiple_of(x * half, 128), half)
        far_rows = pl.ds(pl.multiple_of(other * half, 128), half)
        mine = tokens[...]
        for load in loads[:3]:
            load.wait()
        keys = mul(mine, key_w[own_rows, :])
        values = mul(mine, value_w[own_rows, :])
        queries = mul(mine, query_w[own_rows, :])
        rates = mul(mine, rate_w[:, own_rows], NT)
        token_copy.wait_recv()
        far = other_tokens[...]
        keys = (keys + mul(far, key_w[far_rows, :])).astype(BF16)
        values = (values + mul(far, value_w[far_rows, :])).astype(BF16)
        rates = rates + mul(far, rate_w[:, far_rows], NT)
        rates = jnp.maximum(rates, 0.0) + jnp.log1p(jnp.exp(-jnp.abs(rates)))
        rates = rates * jnp.where(chip < contributors, 1.0, 0.0)
        queries = (queries + mul(far, query_w[far_rows, :])).astype(BF16)

        def packed(head):
            cols = slice(head * width, (head + 1) * width)
            error = (-rates[:, head : head + 1] * values[:, cols].astype(F32)).astype(BF16)
            return jnp.concatenate((keys[:, cols], values[:, cols], queries[:, cols], error), 1)

        first, second = packed(0), packed(1)
        mate_out[...] = jnp.where(core == 0, second, first)
        core_rows = pl.ds(pl.multiple_of(core * rows, 128), rows)
        mate_rows = pl.ds(pl.multiple_of((1 - core) * rows, 128), rows)
        mate_copy = remote(mate_out, both.at[core_rows, :], mate_send.at[0], mate_recv.at[0], (mate, x))
        mate_copy.start()
        both[core_rows, :] = jnp.where(core == 0, first, second)
        for load in loads[3:]:
            load.wait()
        out_copy = remote(
            out_w.at[:, pl.ds(pl.multiple_of(other * half, 128), half)], other_out_w, out_send, out_recv, (t, other)
        )
        out_copy.start()
        lowered = [fast[m].astype(BF16) for m in range(MATRICES)]
        remote(mate_out, both.at[mate_rows, :], mate_send.at[0], mate_recv.at[0], (mate, x)).wait_recv()
        remote(
            view_out,
            both_views.at[:, pl.ds(pl.multiple_of((1 - core) * rows, 128), rows)],
            mate_send.at[1],
            mate_recv.at[1],
            (mate, x),
        ).wait_recv()

        span_rows = 2 * rows
        window[span, 0:span_rows, :] = both[:, 0 : 2 * width]
        window[span, span_rows : span_rows + 16, :] = jnp.concatenate(
            (both_views[...], jnp.zeros((16, 2 * width - span_rows), BF16)), 1
        )

        def reduce_copy(m):
            return remote(
                partial.at[m],
                arrived.at[chip],
                reduce_send.at[m],
                reduce_recv.at[chip],
                (tok_of(core * MATRICES + m), x),
            )

        def hand_over(m, value):
            partial[m] = value.astype(BF16)
            owner = core * MATRICES + m

            @pl.when(owner == chip)
            def _():
                own_total[...] = value

            @pl.when(owner != chip)
            def _():
                reduce_copy(m).start()

        @pl.when(chip < contributors)
        def _():
            keys_n = normalize(both[:, 0:width])
            error = both[:, 3 * width : 4 * width]
            gate = mul(keys_n, lowered[0])
            upward = mul(keys_n, lowered[1])
            logistic = sigmoid(gate)
            active = gate * logistic
            hand_over(2, mul(error, (active * upward).astype(BF16), TN))
            back = mul(error, lowered[2])
            hand_over(1, mul(keys_n, (back * active).astype(BF16), TN))
            grad_gate = (back * upward * logistic * (1.0 + gate * (1.0 - logistic))).astype(BF16)
            hand_over(0, mul(keys_n, grad_gate, TN))

        def window_copy(offset):
            return remote(
                window.at[span],
                window.at[span - offset],
                window_send.at[span + offset],
                window_recv.at[span - offset],
                (tok_of(chip + offset), x),
            )

        offsets = [o for o in range(-span, span + 1) if o]
        @pl.when(chip < contributors)
        def _():
            for m in range(MATRICES):

                @pl.when(chip != core * MATRICES + m)
                def _(m=m):
                    reduce_copy(m).wait_send()

        for offset in offsets:
            inside = (chip + offset >= 0) & (chip + offset < chips)

            @pl.when(inside)
            def _(offset=offset):
                window_copy(offset).start()

            @pl.when(jnp.logical_not(inside))
            def _(offset=offset):
                window[span + offset, 0:span_rows, :] = jnp.zeros((span_rows, 2 * width), BF16)
                window[span + offset, span_rows : span_rows + 16, :] = jnp.full((16, 2 * width), -1.0, BF16)

        index = chip - core * MATRICES
        owns = (index >= 0) & (index < MATRICES)

        across = chip + 1 - 2 * lax.rem(chip, 2)

        def fresh_copy(k):
            target = across if k is None else lax.rem(chip + 2 * k, chips)
            return remote(
                fresh.at[index],
                fresh.at[index],
                fresh_send.at[0 if k is None else k],
                fresh_recv.at[index],
                (tok_of(target), x),
            )

        def forward_copy(m):
            return remote(
                fresh.at[m], fresh.at[m], forward_send.at[m], fresh_recv.at[m], (tok_of(across), x)
            )

        def forwards(m):
            owner = core * MATRICES + m
            return (chip != owner) & (lax.rem(chip + owner, 2) == 0)

        @pl.when(owns)
        def _():
            @pl.loop(1, contributors)
            def _(k):
                source = lax.rem(chip + k, contributors)
                remote(
                    partial.at[0], arrived.at[source], reduce_send.at[0], reduce_recv.at[source], (mate, x)
                ).wait_recv()
                own_total[...] += arrived[source].astype(F32)

            pace = jnp.where(core == 0, step[0], step[1])
            updated = (fast[index] - pace * orthogonalize(own_total[...])).astype(BF16)
            fresh[index] = updated

            @pl.loop(1, chips // 2)
            def _(k):
                fresh_copy(k).start()

            fresh_copy(None).start()

        own_queries = both[:, 2 * width : 3 * width]
        own_views = both_views[0:1, :].astype(F32)
        diagonal = lax.broadcasted_iota(jnp.int32, (span_rows, span_rows), 0) == lax.broadcasted_iota(
            jnp.int32, (span_rows, span_rows), 1
        )
        column_views = jnp.sum(jnp.where(diagonal, own_views, 0.0), axis=1, keepdims=True)
        scores = []
        for offset in sorted(range(-span, span + 1), key=abs):
            slot = span + offset
            if offset:

                @pl.when((chip + offset >= 0) & (chip + offset < chips))
                def _(slot=slot):
                    remote(
                        window.at[span], window.at[slot], window_send.at[slot], window_recv.at[slot], (mate, x)
                    ).wait_recv()

            score = mul(own_queries, window[slot, 0:span_rows, 0:width], NT) * width ** (-0.5)
            near = window[slot, span_rows : span_rows + 16, 0:span_rows].astype(F32)[0:1, :]
            scores.append((slot, jnp.where(column_views == near, score, masked_score)))
        peak = scores[0][1].max(axis=1, keepdims=True)
        for _, score in scores[1:]:
            peak = jnp.maximum(peak, score.max(axis=1, keepdims=True))
        weights = [(slot, jnp.exp(score - peak)) for slot, score in scores]
        denominator = sum(w.sum(axis=1, keepdims=True) for _, w in weights)
        attended = sum(
            mul((w / denominator).astype(BF16), window[slot, 0:span_rows, width : 2 * width]) for slot, w in weights
        )

        queries_n = normalize(own_queries)
        for m in range(MATRICES):

            @pl.when(forwards(m))
            def _(m=m):
                forward_copy(m).wait_recv()
                forward_copy(m).start()

        for m in range(MATRICES):

            @pl.when(lax.rem(chip + core * MATRICES + m, 2) == 1)
            def _(m=m):
                forward_copy(m).wait_recv()

        gate = mul(queries_n, fresh[0])
        upward = mul(queries_n, fresh[1])
        product = (gate * sigmoid(gate) * upward).astype(BF16)
        mixed = (attended + mul(product, fresh[2], NT)).astype(BF16)

        mixed_out[...] = mixed
        copies = [
            remote(mixed_out.at[where, :], mixed_in.at[i], mixed_send.at[i], mixed_recv.at[i], who)
            for i, (where, who) in enumerate(
                ((mate_rows, group[0]), (core_rows, group[1]), (mate_rows, group[2]))
            )
        ]
        for i in (1, 2, 0):
            copies[i].start()
        out_copy.wait_recv()
        kept = mixed_out[core_rows, :]
        copies[0].wait_recv()

        def side_by_side(a, b):
            return jnp.where(core == 0, jnp.concatenate((a, b), 1), jnp.concatenate((b, a), 1))

        total = mul(side_by_side(kept, mixed_in[0]), out_w[:, pl.ds(pl.multiple_of(x * half, 128), half)])
        copies[1].wait_recv()
        copies[2].wait_recv()
        total = total + mul(side_by_side(mixed_in[1], mixed_in[2]), other_out_w[...])
        result[...] = total.astype(BF16)

        token_copy.wait_send()
        view_copy.wait_send()
        mate_copy.wait_send()
        out_copy.wait_send()
        for copy in copies:
            copy.wait_send()

        for offset in offsets:

            @pl.when((chip + offset >= 0) & (chip + offset < chips))
            def _(offset=offset):
                window_copy(offset).wait_send()

        @pl.when(owns)
        def _():
            @pl.loop(1, chips // 2)
            def _(k):
                fresh_copy(k).wait_send()

            fresh_copy(None).wait_send()

        for m in range(MATRICES):

            @pl.when(forwards(m))
            def _(m=m):
                forward_copy(m).wait_send()

    return kernel


def body(
    tokens, view_ids, query_weight, key_weight, value_weight, out_weight,
    rate_weight, fast_gate, fast_up, fast_down, step_size,
):
    tok_count = lax.axis_size("tok")
    chips = tok_count // 2
    span = min(8, tok_count // 4) // 2
    contributors = 3 * tok_count // 8
    rows, half = tokens.shape
    width, hidden = fast_gate.shape[1:]
    slots = 2 * span + 1
    vmem = pl.BlockSpec(memory_space=pltpu.VMEM)
    anywhere = pl.BlockSpec(memory_space=pltpu.HBM)
    dma = pltpu.SemaphoreType.DMA
    matrix = (width, hidden)
    return pl.pallas_call(
        make_kernel(tok_count, span, contributors),
        out_shape=jax.ShapeDtypeStruct((rows, half), BF16),
        in_specs=[vmem, vmem, anywhere, anywhere, anywhere, anywhere, vmem, anywhere, anywhere, anywhere,
                  pl.BlockSpec(memory_space=pltpu.SMEM)],
        out_specs=vmem,
        scratch_shapes=[
            pltpu.VMEM(query_weight.shape, BF16),
            pltpu.VMEM(key_weight.shape, BF16),
            pltpu.VMEM(value_weight.shape, BF16),
            pltpu.VMEM(out_weight.shape, BF16),
            pltpu.VMEM((MATRICES,) + matrix, F32),
            dma((7,)),
            pltpu.VMEM((rows, half), BF16),
            dma,
            dma,
            pltpu.VMEM((rows, 4 * width), BF16),
            pltpu.VMEM((2 * rows, 4 * width), BF16),
            pltpu.VMEM((16, 2 * rows), BF16),
            pltpu.VMEM((16, rows), BF16),
            dma((2,)),
            dma((2,)),
            pltpu.VMEM((slots, 2 * rows + 16, 2 * width), BF16),
            dma((slots,)),
            dma((slots,)),
            pltpu.VMEM((MATRICES,) + matrix, BF16),
            pltpu.VMEM((contributors,) + matrix, BF16),
            pltpu.VMEM(matrix, F32),
            dma((MATRICES,)),
            dma((contributors,)),
            pltpu.VMEM((half, half), BF16),
            dma,
            dma,
            pltpu.VMEM((MATRICES,) + matrix, BF16),
            dma((MATRICES,)),
            dma((chips // 2,)),
            dma((MATRICES,)),
            pltpu.VMEM((2 * rows, width), BF16),
            pltpu.VMEM((3, rows, width), BF16),
            dma((3,)),
            dma((3,)),
        ],
        compiler_params=pltpu.CompilerParams(
            collective_id=0, has_side_effects=True, vmem_limit_bytes=62 * 1024 * 1024
        ),
    )(
        tokens, view_ids.reshape(1, rows), query_weight, key_weight, value_weight, out_weight,
        rate_weight.T, fast_gate, fast_up, fast_down, step_size,
    )


def solution(mesh):
    placed = (
        P("tok", "head"),
        P("tok"),
        P(None, "head"),
        P(None, "head"),
        P(None, "head"),
        P("head", None),
        P(None, "head"),
        P("head", None, None),
        P("head", None, None),
        P("head", None, None),
        P("head"),
    )
    return jax.shard_map(
        body, mesh=mesh, in_specs=placed, out_specs=P("tok", "head"), check_vma=False
    )
```
